128 devices in a mesh: dp: 16 (over y, z), frame: 8 (over x, core).
Axes of the slice: x: 4, y: 4, z: 4, core: 2. Of those that a mesh axis runs over, the one named last changes fastest.
Arguments:
- video: bfloat16 [32, 16, 12, 20, 1024], P('dp', 'frame'), may hold values from -6 to 6
- norm_gain: float32 [1024], replicated, may hold values from 0.5 to 1.5
- spatial_weight: bfloat16 [9, 1024, 1024], P(None, 'dp'), may hold values from -0.0625 to 0.0625
- spatial_bias: float32 [1024], replicated, may hold values from -3 to 3
- temporal_weight: bfloat16 [3, 1024, 1024], P(None, 'dp'), may hold values from -0.109375 to 0.109375
Outputs:
- result: bfloat16 [32, 16, 12, 20, 1024], P('dp', 'frame')
The draws below stay inside these ranges and needn't reach their ends.
All inputs are finite; a program needn't handle non-finite values.
Results may differ from the reference program's by a relative error of at most 0.0033.
Values may be sent and summed in bfloat16 or wider, within the bound.
No kernel may reach another device: no remote copies, remote signals or barrier semaphores. Data moves between devices by JAX's collectives and lax.ppermute only.
A program may use at most 128 MiB of HBM per device.

```python
import jax
import jax.numpy as jnp
from jax import lax

C = 1024
HEIGHT = 12
WIDTH = 20
BATCH = 32
FRAMES = 16


def shard_levels(key, dims, shards, smallest, top_value):
    loudness, own = 1.0, jax.random.fold_in(key, 6)
    for dim, parts in shards:
        heights = jnp.exp(jax.random.uniform(jax.random.fold_in(own, dim), (parts,), jnp.float32, smallest / len(shards), top_value / len(shards)))
        loudness = loudness * jnp.repeat(heights, dims[dim] // parts).reshape([-1 if axis == dim else 1 for axis in range(len(dims))])
    return loudness


def normal_values(rng, shape, deviation, bound, pieces=(), kind=jnp.bfloat16):
    entries = deviation * jax.random.normal(rng, shape, jnp.float32)
    if pieces:
        entries = entries * shard_levels(rng, shape, pieces, -0.22, 0.18)
    return jnp.clip(entries, -bound, bound).astype(kind)


def setup_inputs(seed: int = 0) -> dict:
    streams_of = jax.random.split(jax.random.key(seed), 6)
    video = normal_values(streams_of[0], (BATCH, FRAMES, HEIGHT, WIDTH, C), 1.0, 6.0, ((0, 16), (1, 8)))
    norm_gain = jnp.clip(1.0 + 0.1 * jax.random.normal(streams_of[1], (C,), jnp.float32), 0.5, 1.5)
    spatial_weight = normal_values(streams_of[2], (9, C, C), (9 * C) ** -0.5, 0.0625, ((1, 16),))
    spatial_bias = normal_values(streams_of[3], (C,), 0.5, 3.0, (), jnp.float32)
    temporal_weight = normal_values(streams_of[4], (3, C, C), (3 * C) ** -0.5, 0.109375, ((1, 16),))
    return dict(video=video, norm_gain=norm_gain, spatial_weight=spatial_weight, spatial_bias=spatial_bias, temporal_weight=temporal_weight)


def one_video(clip, norm_gain, spatial_weight, spatial_bias, temporal_weight):
    widened = clip.astype(jnp.float32)
    scaled = widened * lax.rsqrt(lax.optimization_barrier(jnp.mean(widened * widened, axis=-1, keepdims=True)) + 1e-06) * norm_gain
    active = jax.nn.silu(scaled).astype(jnp.bfloat16)
    padded = jnp.pad(active, ((0, 0), (1, 1), (1, 1), (0, 0)))
    total = jnp.zeros((FRAMES * HEIGHT * WIDTH, C), jnp.float32)
    for row_off in range(3):
        for col_off in range(3):
            window = padded[:, row_off:row_off + HEIGHT, col_off:col_off + WIDTH, :].reshape(-1, C)
            total = total + jnp.dot(window, spatial_weight[3 * row_off + col_off], preferred_element_type=jnp.float32)
    hidden = jax.nn.silu(total + spatial_bias).astype(jnp.bfloat16).reshape(FRAMES, HEIGHT * WIDTH, C)
    extended = jnp.pad(hidden, ((1, 1), (0, 0), (0, 0)))
    temporal = jnp.zeros((FRAMES * HEIGHT * WIDTH, C), jnp.float32)
    for offset in range(3):
        temporal = temporal + jnp.dot(extended[offset:offset + FRAMES].reshape(-1, C), temporal_weight[offset], preferred_element_type=jnp.float32)
    return (widened + temporal.reshape(clip.shape)).astype(jnp.bfloat16)

def reference(video, norm_gain, spatial_weight, spatial_bias, temporal_weight):
    return lax.map(lambda clip: one_video(clip, norm_gain, spatial_weight, spatial_bias, temporal_weight), video)
```

```python
import functools

import jax
import jax.numpy as jnp
from jax import lax
from jax.experimental import pallas as pl
from jax.experimental.pallas import tpu as pltpu
from jax.sharding import Mesh
from jax.sharding import PartitionSpec as P

EPSILON = 1e-06
F32, BF16 = jnp.float32, jnp.bfloat16
MIB = 2**20

ROWS, COLS, SLOTS = 12, 20, 8
LINE = COLS * SLOTS
POINTS = ROWS * LINE


def silu(v):
    return v / (1.0 + jnp.exp(-v))


def specs(*kinds):
    places = {"s": pltpu.SMEM, "v": pltpu.VMEM, "h": pl.ANY}
    return [pl.BlockSpec(memory_space=places[kind]) for kind in kinds]


def params(mib):
    return pltpu.CompilerParams(vmem_limit_bytes=mib * MIB)


def cost(flops, bytes_accessed):
    return pl.CostEstimate(flops=flops, bytes_accessed=bytes_accessed, transcendentals=0)


def pack_kernel(where, spatial, temporal, unit_a, unit_b):
    core = where[3]
    source = lax.broadcasted_iota(jnp.int32, (256, 128), 0)
    target = lax.broadcasted_iota(jnp.int32, (256, 128), 1)
    wanted = (target >> 5) * 64 + (target & 31) + core * 32
    pick = jnp.where(source == wanted, 1.0, 0.0).astype(BF16)
    for part in range(4):
        unit = (unit_a, unit_b)[part // 2]
        columns = spatial[:, :, part * 256 : (part + 1) * 256].reshape(576, 256)
        kept = jnp.dot(columns, pick, preferred_element_type=F32).astype(BF16)
        unit[0:576, (part % 2) * 128 : (part % 2 + 1) * 128] = kept
    for tap in range(3):
        rows = temporal[tap, pl.ds(pl.multiple_of(core * 32, 32), 32), :]
        for part in range(4):
            unit = (unit_a, unit_b)[part // 2]
            start = 576 + (part % 2) * 96 + tap * 32
            unit[start : start + 32, :] = rows[:, part * 256 : (part + 1) * 256]


def pack(where, spatial, temporal):
    unit = jax.ShapeDtypeStruct((768, 256), BF16)
    return pl.pallas_call(
        pack_kernel,
        out_shape=(unit, unit),
        in_specs=specs("s", "v", "v"),
        out_specs=specs("v", "v"),
        compiler_params=params(16),
        cost_estimate=cost(10**9, 3 * 10**6),
    )(where, spatial, temporal)


def arrange_kernel(where, own, other, gain, wide_a, core_a, wide_b, core_b, active):
    core = where[3]
    scale = gain[...]
    for relative, video in ((0, own), (1, other)):
        owner = core if relative == 0 else 1 - core
        for index in range(2):
            for frame in range(2):
                slot = (2 * owner + frame) * 2 + index

                def line(i, carry, video=video, index=index, frame=frame, slot=slot):
                    values = video[index, frame, i].astype(F32)
                    mean = jnp.mean(values * values, axis=-1, keepdims=True)
                    scaled = values * lax.rsqrt(mean + EPSILON) * scale
                    scaled = silu(scaled)
                    for part in range(8):
                        active[part, pl.ds(i * LINE + slot, COLS, stride=SLOTS), :] = scaled[
                            :, part * 128 : (part + 1) * 128
                        ]
                    return carry

                lax.fori_loop(0, ROWS, line, 0, unroll=2)

    low = lax.broadcasted_iota(jnp.int32, (LINE, 128), 1) < 64
    edge = jnp.zeros((SLOTS, 256), F32)

    def put(wide, narrow, block, i, value):
        narrow[block, i + 1] = value.astype(BF16)
        wide[block, i + 1] = jnp.concatenate([edge, value, edge], axis=0).astype(BF16)

    def spread(i, carry):
        lines = [active[part, pl.ds(i * LINE, LINE), :] for part in range(8)]
        turned = [pltpu.roll(value, 64, 1) for value in lines]
        for y in range(4):
            put(wide_b, core_b, y, i, jnp.concatenate([lines[2 * y], lines[2 * y + 1]], axis=1))
        for z in range(4):
            halves = []
            for y in (0, 2):
                first, second = y * 2 + z // 2, (y + 1) * 2 + z // 2
                if z % 2 == 0:
                    halves.append(jnp.where(low, lines[first], turned[second]))
                else:
                    halves.append(jnp.where(low, turned[first], lines[second]))
            put(wide_a, core_a, z, i, jnp.concatenate(halves, axis=1))
        return carry

    lax.fori_loop(0, ROWS, spread, 0)
    for block in range(4):
        for i in (0, ROWS + 1):
            for ref in (wide_a, core_a, wide_b, core_b):
                ref[block, i] = jnp.zeros(ref.shape[2:], BF16)


def arrange(where, own, other, gain):
    wide = jax.ShapeDtypeStruct((4, ROWS + 2, LINE + 16, 256), BF16)
    narrow = jax.ShapeDtypeStruct((4, ROWS + 2, LINE, 256), BF16)
    return pl.pallas_call(
        arrange_kernel,
        out_shape=(wide, narrow, wide, narrow),
        in_specs=specs("s", "v", "v", "v"),
        out_specs=specs("v", "v", "v", "v"),
        scratch_shapes=[pltpu.VMEM((8, POINTS, 128), F32)],
        compiler_params=params(52),
        cost_estimate=cost(10**9, 25 * 10**6),
    )(where, own, other, gain)


def stack_kernel(*refs):
    units, (sa, ta, sb, tb), sem = refs[:8], refs[8:12], refs[12]
    copies = []
    for index in range(8):
        spatial, temporal = ((sa, ta), (sb, tb))[index // 4]
        slot = index % 4
        copies.append((units[index].at[pl.ds(0, 576)], spatial.at[slot]))
        copies.append((units[index].at[pl.ds(576, 192)], temporal.at[slot]))
    started = []
    for number, (source, target) in enumerate(copies):
        copy = pltpu.make_async_copy(source, target, sem.at[number])
        copy.start()
        started.append(copy)
    for copy in started:
        copy.wait()


def stack(units):
    spatial = jax.ShapeDtypeStruct((4, 576, 256), BF16)
    temporal = jax.ShapeDtypeStruct((4, 192, 256), BF16)
    return pl.pallas_call(
        stack_kernel,
        out_shape=(spatial, temporal, spatial, temporal),
        in_specs=specs(*"hhhhhhhh"),
        out_specs=specs(*"hhhh"),
        scratch_shapes=[pltpu.SemaphoreType.DMA((16,))],
        compiler_params=params(8),
        cost_estimate=cost(0, 6 * 10**6),
    )(*units)


def conv_kernel(step, *refs):
    first, last = step == 0, step == 3
    refs = list(refs)
    where, *inputs = refs[:7]
    refs = refs[7:]
    wide_hbm, narrow_hbm, spatial_hbm = (inputs[0], inputs[2]), (inputs[1], inputs[3]), inputs[4:6]
    sums_hbm = None
    if not first:
        sums_hbm, refs = refs[:2], refs[2:]
    if last:
        bias, refs = refs[0], refs[1:]
        hidden, lower, upper = refs[:3]
        refs = refs[3:]
    else:
        out, refs = refs[:2], refs[2:]
    wide, narrow, pieces, kernel, sums, sem = refs[:6]
    sides = refs[6] if last else None
    y, z, core = where[0], where[1], where[3]
    turn = 2 * core - 1
    mine = (z, y)
    across = (y, z)
    waits = []
    for colour in range(2):
        block = (mine[colour] + turn * step + 4) & 3
        copies = [
            pltpu.make_async_copy(spatial_hbm[colour], pieces.at[colour], sem.at[colour, 0]),
            pltpu.make_async_copy(wide_hbm[colour].at[block], wide.at[colour], sem.at[colour, 1]),
            pltpu.make_async_copy(narrow_hbm[colour].at[block], narrow.at[colour], sem.at[colour, 2]),
        ]
        if not first:
            copies.append(pltpu.make_async_copy(sums_hbm[colour], sums.at[colour], sem.at[colour, 3]))
        for copy in copies:
            copy.start()
        waits.append(copies)
    outs = []
    for colour in range(2):
        for copy in waits[colour]:
            copy.wait()
        for slot in range(4):
            place = (across[colour] + turn * slot + 4) & 3
            for tap in range(9):
                kernel[pl.ds(pl.multiple_of(tap * 256 + place * 64, 64), 64), :] = pieces[
                    colour, slot, tap * 64 : (tap + 1) * 64, :
                ]

        lines = 4

        def part(group, carry, colour=colour):
            i = group * lines
            total = None
            for tap in range(9):
                dy, dx = tap // 3, tap % 3
                if dx == 1:
                    window = narrow[colour, pl.ds(i + dy, lines), :, :]
                else:
                    window = wide[colour, pl.ds(i + dy, lines), dx * 8 : dx * 8 + LINE, :]
                product = jnp.dot(
                    window.reshape(lines * LINE, 256),
                    kernel[tap * 256 : (tap + 1) * 256, :],
                    preferred_element_type=F32,
                )
                total = product if total is None else total + product
            rows = pl.ds(pl.multiple_of(i * LINE, lines * LINE), lines * LINE)
            if not first:
                total = total + sums[colour, rows, :]
            if last:
                total = silu(total + bias[:, colour * 256 : (colour + 1) * 256])
                hidden[rows, colour * 256 : (colour + 1) * 256] = total.astype(BF16)
                for half in range(2):
                    sides[colour * 2 + half, rows, :] = total[:, half * 128 : (half + 1) * 128]
            else:
                sums[colour, rows, :] = total
            return carry

        lax.fori_loop(0, ROWS // lines, part, 0)
        if last:
            for half in range(2):
                columns = slice(colour * 256 + half * 128, colour * 256 + (half + 1) * 128)
                for index in range(2):
                    for target, slot in ((lower, index), (upper, 6 + index)):
                        target[index, :, columns] = sides[
                            colour * 2 + half, pl.ds(slot, ROWS * COLS, stride=SLOTS), :
                        ].astype(BF16)
        else:
            copy = pltpu.make_async_copy(sums.at[colour], out[colour], sem.at[colour, 4])
            copy.start()
            outs.append(copy)
    for copy in outs:
        copy.wait()


def conv(step, where, active, spatial, sums=None, bias=None):
    operands = [where, *active, *spatial]
    kinds = "shhhhhh"
    if step > 0:
        operands += sums
        kinds += "hh"
    if step == 3:
        operands.append(bias)
        kinds += "v"
        side = jax.ShapeDtypeStruct((2, ROWS * COLS, 512), BF16)
        out_shape = (jax.ShapeDtypeStruct((POINTS, 512), BF16), side, side)
        out_specs = specs(*"vvv")
    else:
        total = jax.ShapeDtypeStruct((POINTS, 256), F32)
        out_shape, out_specs = (total, total), specs(*"hh")
    return pl.pallas_call(
        functools.partial(conv_kernel, step),
        out_shape=out_shape,
        in_specs=specs(*kinds),
        out_specs=out_specs,
        scratch_shapes=[
            pltpu.VMEM((2, ROWS + 2, LINE + 16, 256), BF16),
            pltpu.VMEM((2, ROWS + 2, LINE, 256), BF16),
            pltpu.VMEM((2, 4, 576, 256), BF16),
            pltpu.VMEM((2304, 256), BF16),
            pltpu.VMEM((2, POINTS, 256), F32),
            pltpu.SemaphoreType.DMA((2, 5)),
        ]
        + ([pltpu.VMEM((4, POINTS, 128), F32)] if step == 3 else []),
        compiler_params=params(40),
        cost_estimate=cost(2 * 2 * POINTS * 2304 * 256, 18 * 10**6),
    )(*operands)


def temporal_kernel(where, hidden, before, after, *refs):
    blocks, (mine, theirs, plain, kernel, pieces, shifted, total, sem) = refs[:8], refs[8:]
    y, z, core = where[0], where[1], where[3]
    turn = 2 * core - 1
    copies = []
    for number in range(8):
        copy = pltpu.make_async_copy(blocks[number], pieces.at[number], sem.at[number])
        copy.start()
        copies.append(copy)
    slot = lax.broadcasted_iota(jnp.int32, (LINE, 128), 0) & 7
    zero = jnp.zeros((SLOTS, 128), F32)
    for part in range(4):
        columns = slice(part * 128, (part + 1) * 128)

        def move(i, carry, part=part, columns=columns):
            rows = pl.ds(pl.multiple_of(i * LINE, LINE), LINE)
            values = hidden[rows, columns].astype(F32)
            plain[0, rows, :] = jnp.where(slot >= 2, pltpu.roll(values, 2, 0), 0.0)
            plain[1, rows, :] = jnp.where(slot < 6, pltpu.roll(values, LINE - 2, 0), 0.0)
            return carry

        lax.fori_loop(0, ROWS, move, 0)
        for index in range(2):
            plain[0, pl.ds(index, ROWS * COLS, stride=SLOTS), :] = before[index, :, columns].astype(F32)
            plain[1, pl.ds(6 + index, ROWS * COLS, stride=SLOTS), :] = after[index, :, columns].astype(F32)
        shifted[0, :, columns] = plain[0].astype(BF16)
        shifted[1, :, columns] = plain[1].astype(BF16)
    for copy in copies:
        copy.wait()
    for number in range(8):
        colour, step = number // 4, number % 4
        for unit in range(4):
            fixed, moving = (unit, step) if colour == 0 else (step, unit)
            row, column = (y + turn * fixed + 4) & 3, (z + turn * moving + 4) & 3
            place = pl.multiple_of((row * 4 + column) * 32, 32)
            for tap in range(3):
                for half in range(2):
                    start = half * 96 + tap * 32
                    kernel[tap, pl.ds(place, 32), (colour * 2 + half) * 256 : (colour * 2 + half + 1) * 256] = pieces[
                        number, unit, start : start + 32, :
                    ]

    for part in range(4):
        columns = slice(part * 256, (part + 1) * 256)

        def multiply(group, carry, part=part, columns=columns):
            rows = pl.ds(pl.multiple_of(group * 640, 640), 640)
            value = jnp.dot(hidden[rows, :], kernel[1, :, columns], preferred_element_type=F32)
            value = value + jnp.dot(shifted[0, rows, :], kernel[0, :, columns], preferred_element_type=F32)
            value = value + jnp.dot(shifted[1, rows, :], kernel[2, :, columns], preferred_element_type=F32)
            for half in range(2):
                total[part * 2 + half, rows, :] = value[:, half * 128 : (half + 1) * 128]
            return carry

        lax.fori_loop(0, 3, multiply, 0)

    for index in range(2):
        for frame in range(2):
            for target, owner in ((theirs, 1 - core), (mine, core)):
                start = (2 * owner + frame) * 2 + index

                def line(i, carry, target=target, start=start, index=index, frame=frame):
                    for part in range(8):
                        target[index, frame, i, :, part * 128 : (part + 1) * 128] = total[
                            part, pl.ds(i * LINE + start, COLS, stride=SLOTS), :
                        ].astype(target.dtype)
                    return carry

                lax.fori_loop(0, ROWS, line, 0)


def temporal(where, hidden, before, after, blocks):
    shape = (2, 2, ROWS, COLS, 1024)
    return pl.pallas_call(
        temporal_kernel,
        out_shape=(jax.ShapeDtypeStruct(shape, F32), jax.ShapeDtypeStruct(shape, BF16)),
        in_specs=specs("s", "v", "v", "v", *"hhhhhhhh"),
        out_specs=specs("v", "v"),
        scratch_shapes=[
            pltpu.VMEM((2, POINTS, 128), F32),
            pltpu.VMEM((3, 512, 1024), BF16),
            pltpu.VMEM((8, 4, 192, 256), BF16),
            pltpu.VMEM((2, POINTS, 512), BF16),
            pltpu.VMEM((8, POINTS, 128), F32),
            pltpu.SemaphoreType.DMA((8,)),
        ],
        compiler_params=params(52),
        cost_estimate=cost(2 * 3 * POINTS * 512 * 1024, 12 * 10**6),
    )(where, hidden, before, after, *blocks)


def finish_kernel(video, mine, received, result):
    result[...] = (video[...].astype(F32) + mine[...] + received[...].astype(F32)).astype(BF16)


def finish(video, mine, received):
    block = pl.BlockSpec((1, 1, ROWS, COLS, 1024), lambda i: (i // 2, i % 2, 0, 0, 0))
    return pl.pallas_call(
        finish_kernel,
        grid=(4,),
        out_shape=jax.ShapeDtypeStruct(video.shape, BF16),
        in_specs=[block] * 3,
        out_specs=block,
        compiler_params=params(24),
        cost_estimate=cost(3 * 10**6, 10 * 10**6),
    )(video, mine, received)


def ring(value, axis):
    count = lax.axis_size(axis)
    pairs = [(i * 2, (i + 1) % count * 2) for i in range(count)]
    pairs += [(i * 2 + 1, (i - 1) % count * 2 + 1) for i in range(count)]
    return lax.ppermute(value, (axis, "core"), pairs)


def shards(video, norm_gain, spatial_weight, spatial_bias, temporal_weight):
    where = jnp.stack([lax.axis_index(axis) for axis in ("y", "z", "x", "core")]).astype(jnp.int32)
    swap = [(0, 1), (1, 0)]
    other = lax.ppermute(video, "core", swap)
    unit_a, unit_b = pack(where, spatial_weight, temporal_weight)
    units_a, units_b = [unit_a], [unit_b]
    for _ in range(3):
        units_a.append(ring(units_a[-1], "y"))
        units_b.append(ring(units_b[-1], "z"))
    active = arrange(where, video, other, norm_gain.reshape(1, 1024))
    bias = spatial_bias.reshape(16, 2, 32)[:, where[3], :].reshape(1, 512)

    sa, ta, sb, tb = stack(units_a + units_b)
    spatial, later = [(sa, sb)], [(ta, tb)]
    for _ in range(3):
        spatial.append((ring(spatial[-1][0], "z"), ring(spatial[-1][1], "y")))
        later.append((ring(later[-1][0], "z"), ring(later[-1][1], "y")))

    sums = None
    for step in range(3):
        sums = conv(step, where, active, spatial[step], sums)
    hidden, lower, upper = conv(3, where, active, spatial[3], sums, bias)
    count = lax.axis_size("x")
    before = lax.ppermute(upper, "x", [(i, i + 1) for i in range(count - 1)])
    after = lax.ppermute(lower, "x", [(i + 1, i) for i in range(count - 1)])
    blocks = [pair[0] for pair in later] + [pair[1] for pair in later]
    mine, theirs = temporal(where, hidden, before, after, blocks)
    received = lax.ppermute(theirs, "core", swap)
    return finish(video, mine, received)


def solution(mesh):
    parts = Mesh(mesh.devices.reshape(4, 4, 4, 2), ("y", "z", "x", "core"))
    dp, frame = ("y", "z"), ("x", "core")
    in_specs = (
        P(dp, frame, None, None, None),
        P(),
        P(None, dp, None),
        P(),
        P(None, dp, None),
    )
    out_specs = P(dp, frame, None, None, None)
    return jax.shard_map(shards, mesh=parts, in_specs=in_specs, out_specs=out_specs, check_vma=False)
```

```python
import functools

import jax
import jax.numpy as jnp
from jax import lax
from jax.experimental import pallas as pl
from jax.experimental.pallas import tpu as pltpu
from jax.sharding import Mesh
from jax.sharding import PartitionSpec as P

EPSILON = 1e-06
F32, BF16 = jnp.float32, jnp.bfloat16
MIB = 2**20

ROWS, COLS, SLOTS = 12, 20, 8
LINE = COLS * SLOTS
POINTS = ROWS * LINE


def silu(v):
    return v / (1.0 + jnp.exp(-v))


def specs(*kinds):
    places = {"s": pltpu.SMEM, "v": pltpu.VMEM, "h": pltpu.HBM}
    return [pl.BlockSpec(memory_space=places[kind]) for kind in kinds]


def params(mib):
    return pltpu.CompilerParams(vmem_limit_bytes=mib * MIB)


def cost(flops, bytes_accessed):
    return pl.CostEstimate(flops=flops, bytes_accessed=bytes_accessed, transcendentals=0)


def pack_kernel(where, spatial, temporal, unit_a, unit_b):
    core = where[3]
    source = lax.broadcasted_iota(jnp.int32, (256, 128), 0)
    target = lax.broadcasted_iota(jnp.int32, (256, 128), 1)
    wanted = (target >> 5) * 64 + (target & 31) + core * 32
    pick = jnp.where(source == wanted, 1.0, 0.0).astype(BF16)
    for part in range(4):
        unit = (unit_a, unit_b)[part // 2]
        columns = spatial[:, :, part * 256 : (part + 1) * 256].reshape(576, 256)
        kept = jnp.dot(columns, pick, preferred_element_type=F32).astype(BF16)
        unit[0:576, (part % 2) * 128 : (part % 2 + 1) * 128] = kept
    for tap in range(3):
        rows = temporal[tap, pl.ds(pl.multiple_of(core * 32, 32), 32), :]
        for part in range(4):
            unit = (unit_a, unit_b)[part // 2]
            start = 576 + (part % 2) * 96 + tap * 32
            unit[start : start + 32, :] = rows[:, part * 256 : (part + 1) * 256]


def pack(where, spatial, temporal):
    unit = jax.ShapeDtypeStruct((768, 256), BF16)
    return pl.pallas_call(
        pack_kernel,
        out_shape=(unit, unit),
        in_specs=specs("s", "v", "v"),
        out_specs=specs("v", "v"),
        compiler_params=params(16),
        cost_estimate=cost(10**9, 3 * 10**6),
    )(where, spatial, temporal)


def norm_kernel(video, gain, active, flat, lines, plain):
    scale = gain[...]
    for i in range(ROWS):
        values = video[0, 0, i].astype(F32)
        mean = jnp.mean(values * values, axis=-1, keepdims=True)
        lines[i * COLS : (i + 1) * COLS, :] = silu(values * lax.rsqrt(mean + EPSILON) * scale)
        plain[i * COLS : (i + 1) * COLS, :] = values
    active[0] = lines[...].astype(BF16)
    flat[0] = plain[...].astype(BF16)


def norm(video, gain):
    return pl.pallas_call(
        norm_kernel,
        grid=(4,),
        out_shape=(jax.ShapeDtypeStruct((4, ROWS * COLS, 1024), BF16),) * 2,
        in_specs=[
            pl.BlockSpec((1, 1, ROWS, COLS, 1024), lambda i: (i // 2, i % 2, 0, 0, 0)),
            pl.BlockSpec((1, 1024), lambda i: (0, 0)),
        ],
        out_specs=(pl.BlockSpec((1, ROWS * COLS, 1024), lambda i: (i, 0, 0)),) * 2,
        scratch_shapes=[pltpu.VMEM((ROWS * COLS, 1024), F32)] * 2,
        compiler_params=params(24),
        cost_estimate=cost(2 * 10**9, 20 * 10**6),
    )(video, gain)


def spread_kernel(where, own, other, wide_a, wide_b, active):
    core = where[3]
    for relative, source in ((0, own), (1, other)):
        owner = core if relative == 0 else 1 - core
        for index in range(2):
            for frame in range(2):
                slot = (2 * owner + frame) * 2 + index
                for part in range(8):
                    values = source[index * 2 + frame, :, part * 128 : (part + 1) * 128]
                    active[part, pl.ds(slot, ROWS * COLS, stride=SLOTS), :] = values.astype(F32)

    low = lax.broadcasted_iota(jnp.int32, (LINE, 128), 1) < 64
    edge = jnp.zeros((SLOTS, 256), F32)

    def put(wide, block, i, value):
        wide[block, i + 1] = jnp.concatenate([edge, value, edge], axis=0).astype(BF16)

    def line(i, carry):
        lines = [active[part, pl.ds(i * LINE, LINE), :] for part in range(8)]
        for y in range(4):
            put(wide_b, y, i, jnp.concatenate([lines[2 * y], lines[2 * y + 1]], axis=1))
        turned = [pltpu.roll(value, 64, 1) for value in lines]
        for z in range(4):
            halves = []
            for y in (0, 2):
                first, second = y * 2 + z // 2, (y + 1) * 2 + z // 2
                if z % 2 == 0:
                    halves.append(jnp.where(low, lines[first], turned[second]))
                else:
                    halves.append(jnp.where(low, turned[first], lines[second]))
            put(wide_a, z, i, jnp.concatenate(halves, axis=1))
        return carry

    for block in range(4):
        for i in (0, ROWS + 1):
            for ref in (wide_a, wide_b):
                ref[block, i] = jnp.zeros(ref.shape[2:], BF16)
    lax.fori_loop(0, ROWS, line, 0)


def spread(where, own, other):
    wide = jax.ShapeDtypeStruct((4, ROWS + 2, LINE + 16, 256), BF16)
    return pl.pallas_call(
        spread_kernel,
        out_shape=(wide, wide),
        in_specs=specs("s", "v", "v"),
        out_specs=specs("v", "v"),
        scratch_shapes=[pltpu.VMEM((8, POINTS, 128), F32)],
        compiler_params=params(24),
        cost_estimate=cost(2 * 10**9, 25 * 10**6),
    )(where, own, other)


def pick_kernel(where, *refs):
    core = where[3]
    for index in range(2):
        for side in range(2):

            @pl.when(core == side)
            def _(source=refs[index * 2 + side], target=refs[4 + index]):
                target[...] = source[...]


def pick(where, *units):
    unit = jax.ShapeDtypeStruct((768, 256), BF16)
    return pl.pallas_call(
        pick_kernel,
        out_shape=(unit, unit),
        in_specs=specs(*"svvvv"),
        out_specs=specs(*"vv"),
        compiler_params=params(8),
        cost_estimate=cost(0, 2 * 10**6),
    )(where, *units)


def stack_kernel(*refs):
    units, wholes = refs[:8], refs[8:]
    for index in range(8):
        wholes[index // 4][index % 4] = units[index][...]


def stack(units):
    whole = jax.ShapeDtypeStruct((4, 768, 256), BF16)
    return pl.pallas_call(
        stack_kernel,
        out_shape=(whole, whole),
        in_specs=specs(*"vvvvvvvv"),
        out_specs=specs(*"vv"),
        compiler_params=params(12),
        cost_estimate=cost(0, 6 * 10**6),
    )(*units)


def divide_kernel(where, *refs):
    core = where[3]
    for index in range(2):
        for side in range(2):

            @pl.when(core == side)
            def _(source=refs[index * 2 + side], spatial=refs[4 + index], temporal=refs[6 + index]):
                for slot in range(4):
                    spatial[slot] = source[slot, 0:576, :]
                    temporal[slot] = source[slot, 576:768, :]


def divide(where, *wholes):
    spatial = jax.ShapeDtypeStruct((4, 576, 256), BF16)
    temporal = jax.ShapeDtypeStruct((4, 192, 256), BF16)
    return pl.pallas_call(
        divide_kernel,
        out_shape=(spatial, spatial, temporal, temporal),
        in_specs=specs(*"svvvv"),
        out_specs=specs(*"vvvv"),
        compiler_params=params(16),
        cost_estimate=cost(0, 6 * 10**6),
    )(where, *wholes)


def conv_kernel(step, colours, *refs):
    first, last = step == 0, step == 2
    count = len(colours)
    where, refs = refs[0], refs[1:]
    wide, refs = refs[:count], refs[count:]
    pieces, refs = refs[:count], refs[count:]
    if not first:
        sums, refs = refs[:count], refs[count:]
    if last:
        bias, refs = refs[0], refs[1:]
        if colours[0] > 0:
            earlier, refs = refs[:2], refs[2:]
        hidden, lower, upper, kernel, sides = refs
        if colours[0] > 0:
            for ref, source in zip((lower, upper), earlier):
                ref[0] = source[0]
    else:
        out, kernel = refs[:count], refs[count]
    y, z = where[0], where[1]
    mine = (z, y)
    across = (y, z)
    lines = 6
    for number, colour in enumerate(colours):
        block = (mine[colour] - step + 4) & 3
        for slot in range(4):
            place = (across[colour] - slot + 4) & 3
            for tap in range(9):
                kernel[number, pl.ds(pl.multiple_of(tap * 256 + place * 64, 64), 64), :] = pieces[number][
                    slot, tap * 64 : (tap + 1) * 64, :
                ]

        def part(group, carry, number=number, colour=colour, block=block):
            i = group * lines
            total = None
            for tap in range(9):
                dy, dx = tap // 3, tap % 3
                window = wide[number][block, pl.ds(i + dy, lines), dx * 8 : dx * 8 + LINE, :]
                product = jnp.dot(
                    window.reshape(lines * LINE, 256),
                    kernel[number, tap * 256 : (tap + 1) * 256, :],
                    preferred_element_type=F32,
                )
                total = product if total is None else total + product
            rows = pl.ds(pl.multiple_of(i * LINE, lines * LINE), lines * LINE)
            if not first:
                total = total + sums[number][rows, :]
            if last:
                total = silu(total + bias[:, colour * 256 : (colour + 1) * 256])
                hidden[rows, :] = total.astype(BF16)
                for half in range(2):
                    sides[half, rows, :] = total[:, half * 128 : (half + 1) * 128]
            else:
                out[number][rows, :] = total
            return carry

        lax.fori_loop(0, ROWS // lines, part, 0)
        if last:
            for half in range(2):
                columns = slice(half * 128, (half + 1) * 128)
                for index in range(2):
                    for ref, slot in ((lower, index), (upper, 6 + index)):
                        values = sides[half, pl.ds(slot, ROWS * COLS, stride=SLOTS), :]
                        ref[colour, index, :, columns] = values.astype(BF16)


def conv(step, colours, where, active, spatial, sums=None, bias=None, sides=()):
    count = len(colours)
    operands = [where, *active, *spatial]
    kinds = "s" + "vv" * count
    scratch = [pltpu.VMEM((count, 2304, 256), BF16)]
    aliases = {}
    if step > 0:
        if step != 2:
            aliases = {len(operands) + number: number for number in range(count)}
        operands += sums
        kinds += "v" * count
    if step == 2:
        operands.append(bias)
        kinds += "v"
        operands += sides
        kinds += "v" * len(sides)
        side = jax.ShapeDtypeStruct((2, 2, ROWS * COLS, 256), BF16)
        out_shape = (jax.ShapeDtypeStruct((POINTS, 256), BF16), side, side)
        out_specs = specs(*"vvv")
        scratch += [pltpu.VMEM((2, POINTS, 128), F32)]
    else:
        total = jax.ShapeDtypeStruct((POINTS, 256), F32)
        out_shape, out_specs = (total,) * count, specs(*"v" * count)
    return pl.pallas_call(
        functools.partial(conv_kernel, step, colours),
        out_shape=out_shape,
        in_specs=specs(*kinds),
        out_specs=out_specs,
        scratch_shapes=scratch,
        input_output_aliases=aliases,
        compiler_params=params(16),
        cost_estimate=cost(4 * 10**9 * count, 12 * 10**6 * count),
    )(*operands)


def shift_kernel(hidden_a, hidden_b, earlier, later):
    slot = lax.broadcasted_iota(jnp.int32, (LINE, 128), 0) & 7
    for part in range(4):
        source, columns = (hidden_a, hidden_b)[part // 2], slice(part % 2 * 128, (part % 2 + 1) * 128)

        def move(i, carry, source=source, columns=columns, part=part):
            rows = pl.ds(pl.multiple_of(i * LINE, LINE), LINE)
            values = source[rows, columns].astype(F32)
            target = slice(part * 128, (part + 1) * 128)
            earlier[rows, target] = jnp.where(slot >= 2, pltpu.roll(values, 2, 0), 0.0).astype(BF16)
            later[rows, target] = jnp.where(slot < 6, pltpu.roll(values, LINE - 2, 0), 0.0).astype(BF16)
            return carry

        lax.fori_loop(0, ROWS, move, 0)


def shift(hidden):
    moved = jax.ShapeDtypeStruct((POINTS, 512), BF16)
    return pl.pallas_call(
        shift_kernel,
        out_shape=(moved, moved),
        in_specs=specs("v", "v"),
        out_specs=specs("v", "v"),
        compiler_params=params(16),
        cost_estimate=cost(10**9, 6 * 10**6),
    )(*hidden)


def place_weights(where, blocks, steps, first_row, targets):
    y, z = where[0], where[1]
    for number, ref in enumerate(blocks):
        colour, step = number % 2, steps[number // 2]
        for unit in range(4):
            fixed, moving = (unit, step) if colour == 0 else (step, unit)
            row, column = (y - fixed + 4) & 3, (z - moving + 4) & 3
            place = pl.ds(pl.multiple_of((row * 4 + column) * 32, 32), 32)
            for half in range(2):
                columns = slice((colour * 2 + half) * 256, (colour * 2 + half + 1) * 256)
                start = first_row + half * 96
                for tap, target in enumerate(targets):
                    target[place, columns] = ref[unit, start + tap * 32 : start + tap * 32 + 32, :]


def ready_kernel(where, *refs):
    blocks, weights = refs[:6], refs[6]
    place_weights(where, blocks, (0, 1, 3), 576, [weights.at[tap] for tap in range(3)])


def ready(where, blocks):
    return pl.pallas_call(
        ready_kernel,
        out_shape=jax.ShapeDtypeStruct((3, 512, 1024), BF16),
        in_specs=specs(*"svvvvvv"),
        out_specs=pl.BlockSpec(memory_space=pltpu.VMEM),
        compiler_params=params(18),
        cost_estimate=cost(0, 5 * 10**6),
    )(where, *blocks)


def centre_kernel(where, hidden_a, hidden_b, earlier, later, weights, block_a, block_b, *refs):
    calm_theirs, calm_mine, rough_theirs, rough_mine, edge, middle, total = refs
    core = where[3]
    edge[0], middle[...], edge[1] = weights[0], weights[1], weights[2]
    place_weights(where, (block_a, block_b), (2,), 0, (edge.at[0], middle, edge.at[1]))
    for part in range(4):
        columns = slice(part * 256, (part + 1) * 256)
        for group in range(2):
            rows = slice(group * 960, (group + 1) * 960)
            value = jnp.dot(hidden_a[rows, :], middle[0:256, columns], preferred_element_type=F32)
            value = value + jnp.dot(hidden_b[rows, :], middle[256:512, columns], preferred_element_type=F32)
            value = value + jnp.dot(earlier[rows, :], edge[0, :, columns], preferred_element_type=F32)
            value = value + jnp.dot(later[rows, :], edge[1, :, columns], preferred_element_type=F32)
            for half in range(2):
                total[part * 2 + half, rows, :] = value[:, half * 128 : (half + 1) * 128]
        for index in range(2):
            for target, owner, frame in (
                (calm_theirs, 1 - core, core),
                (rough_theirs, 1 - core, 1 - core),
                (calm_mine, core, 1 - core),
                (rough_mine, core, core),
            ):
                start = (2 * owner + frame) * 2 + index
                for half in (part * 2, part * 2 + 1):
                    values = total[half, pl.ds(start, ROWS * COLS, stride=SLOTS), :]
                    target[index, :, half * 128 : (half + 1) * 128] = values.astype(target.dtype)


PAIR = (2, ROWS * COLS, 1024)


def centre(where, hidden, moved, weights, blocks):
    wide, narrow = jax.ShapeDtypeStruct(PAIR, F32), jax.ShapeDtypeStruct(PAIR, BF16)
    return pl.pallas_call(
        centre_kernel,
        out_shape=(narrow, wide, wide, wide, jax.ShapeDtypeStruct((2, 512, 1024), BF16)),
        in_specs=specs(*"svvvvvvv"),
        out_specs=specs(*"vvvvv"),
        scratch_shapes=[pltpu.VMEM((512, 1024), BF16), pltpu.VMEM((8, POINTS, 128), F32)],
        compiler_params=params(32),
        cost_estimate=cost(10**10, 12 * 10**6),
    )(where, *hidden, *moved, weights, *blocks)


def edge_kernel(own, where, before, behind, weights, calm, result):
    core = where[3]
    for side, halo in enumerate((before, behind)):

        @pl.when(core == side if own else core != side)
        def _(side=side, halo=halo):
            for index in range(2):
                value = jnp.dot(halo[0, index], weights[side, 0:256, :], preferred_element_type=F32)
                value = value + jnp.dot(halo[1, index], weights[side, 256:512, :], preferred_element_type=F32)
                result[index] = (calm[index] + value).astype(result.dtype)


def edges(own, where, before, behind, weights, calm):
    return pl.pallas_call(
        functools.partial(edge_kernel, own),
        out_shape=jax.ShapeDtypeStruct(PAIR, F32 if own else BF16),
        in_specs=specs(*"svvvv"),
        out_specs=pl.BlockSpec(memory_space=pltpu.VMEM),
        compiler_params=params(24),
        cost_estimate=cost(3 * 10**9, 6 * 10**6),
    )(where, before, behind, weights, calm)


def finish_kernel(where, video, calm_mine, calm_received, rough_mine, rough_received, result, lines):
    core, index = where[3], pl.program_id(0)
    for part in range(8):
        columns = slice(part * 128, (part + 1) * 128)
        for frame, mine, received in (
            (core, rough_mine, rough_received),
            (1 - core, calm_mine, calm_received),
        ):
            value = video[2 * index + frame, :, columns].astype(F32) + (
                mine[index, :, columns] + received[index, :, columns].astype(F32)
            )
            lines[part, pl.ds(frame, ROWS * COLS, stride=2), :] = value
        for i in range(ROWS):
            value = lines[part, i * 2 * COLS : (i + 1) * 2 * COLS, :]
            result[0, i, :, :, columns] = value.astype(BF16).reshape(COLS, 2, 128)


def finish(where, video, *parts):
    shown = pl.pallas_call(
        finish_kernel,
        grid=(2,),
        out_shape=jax.ShapeDtypeStruct((2, ROWS, COLS, 2, 1024), BF16),
        in_specs=specs(*"svvvvv"),
        out_specs=pl.BlockSpec((1, ROWS, COLS, 2, 1024), lambda i: (i, 0, 0, 0, 0)),
        scratch_shapes=[pltpu.VMEM((8, 2 * ROWS * COLS, 128), F32)],
        compiler_params=params(24),
        cost_estimate=cost(3 * 10**6, 10 * 10**6),
    )(where, video, *parts)
    return shown.transpose(0, 3, 1, 2, 4)


def ring(value, axis):
    count = lax.axis_size(axis)
    pairs = [(i * 2, (i + 1) % count * 2) for i in range(count)]
    pairs += [(i * 2 + 1, (i - 1) % count * 2 + 1) for i in range(count)]
    return lax.ppermute(value, (axis, "core"), pairs)


def after(value, *others):
    return lax.optimization_barrier((value, *others))[0]


def step_to(value, axis, distance):
    count = lax.axis_size(axis)
    return lax.ppermute(value, axis, [(i, (i + distance) % count) for i in range(count)])


def shards(video, norm_gain, spatial_weight, spatial_bias, temporal_weight):
    where = jnp.stack([lax.axis_index(axis) for axis in ("y", "z", "x", "core")]).astype(jnp.int32)
    swap = [(0, 1), (1, 0)]
    bias = spatial_bias.reshape(16, 2, 32)[:, where[3], :].reshape(1, 512)
    unit_a, unit_b = pack(where, spatial_weight, temporal_weight)

    a1, b1 = step_to(unit_a, "y", 1), step_to(unit_b, "z", 1)
    a3, b3 = step_to(unit_a, "y", -1), step_to(unit_b, "z", -1)
    own, flat = norm(after(video, unit_a, unit_b, bias), norm_gain.reshape(1, 1024))
    other = lax.ppermute(after(own, a1, b1, a3, b3), "core", swap)
    a2, b2 = pick(where, after(a1, own, flat), a3, b1, b3)
    a2, b2 = ring(a2, "y"), ring(b2, "z")
    whole_a, whole_b = stack((unit_a, a1, a2, a3, unit_b, b1, b2, b3))

    both = (0, 1)
    whole_1 = step_to(whole_a, "z", 1), step_to(whole_b, "y", 1)
    whole_3 = step_to(whole_a, "z", -1), step_to(whole_b, "y", -1)
    active = spread(where, after(own, whole_a), other)
    sums = conv(0, both, where, active, (whole_a, whole_b))
    sa, sb, ta, tb = divide(where, after(whole_1[0], sums[0]), whole_3[0], whole_1[1], whole_3[1])
    sa, sb = ring(sa, "z"), ring(sb, "y")
    sums = conv(1, both, where, active, whole_1, sums)
    sums = conv(3, both, where, active, whole_3, sums)
    weights = ready(where, (whole_a, whole_b, *whole_1, *whole_3))
    ta, tb = ring(after(ta, sums[0]), "z"), ring(after(tb, sums[0]), "y")
    sa, sb = after(sa, sums[0], weights), after(sb, sums[0], weights)
    hidden_a, *sides = conv(2, (0,), where, active[:1], (sa,), sums[:1], bias)
    hidden_b, lower, upper = conv(2, (1,), where, active[1:], (sb,), sums[1:], bias, sides)
    count = lax.axis_size("x")
    before = lax.ppermute(upper, "x", [(i, i + 1) for i in range(count - 1)])
    behind = lax.ppermute(lower, "x", [(i + 1, i) for i in range(count - 1)])
    hidden = hidden_a, hidden_b
    moved = shift(hidden)
    calm_theirs, calm_mine, rough_theirs, rough_mine, weights = centre(where, hidden, moved, weights, (ta, tb))
    calm_received = lax.ppermute(calm_theirs, "core", swap)
    before = after(before, weights)
    sent = edges(False, where, before, behind, weights, rough_theirs)
    rough_received = lax.ppermute(sent, "core", swap)
    rough_mine = edges(True, where, before, behind, weights, after(rough_mine, sent))
    return finish(where, flat, calm_mine, calm_received, rough_mine, rough_received)


def solution(mesh):
    parts = Mesh(mesh.devices.reshape(4, 4, 4, 2), ("y", "z", "x", "core"))
    dp, frame = ("y", "z"), ("x", "core")
    in_specs = (
        P(dp, frame, None, None, None),
        P(),
        P(None, dp, None),
        P(),
        P(None, dp, None),
    )
    out_specs = P(dp, frame, None, None, None)
    return jax.shard_map(shards, mesh=parts, in_specs=in_specs, out_specs=out_specs, check_vma=False)
```

```python
import functools

import jax
import jax.numpy as jnp
from jax import lax
from jax.experimental import pallas as pl
from jax.experimental.pallas import tpu as pltpu
from jax.sharding import Mesh
from jax.sharding import PartitionSpec as P

EPSILON = 1e-06
F32, BF16 = jnp.float32, jnp.bfloat16
MIB = 2**20

ROWS, COLS, SLOTS = 12, 20, 8
LINE = COLS * SLOTS
POINTS = ROWS * LINE


def silu(v):
    return v / (1.0 + jnp.exp(-v))


def specs(*kinds):
    places = {"s": pltpu.SMEM, "v": pltpu.VMEM, "h": pltpu.HBM}
    return [pl.BlockSpec(memory_space=places[kind]) for kind in kinds]


def params(mib):
    return pltpu.CompilerParams(vmem_limit_bytes=mib * MIB)


def cost(flops, bytes_accessed):
    return pl.CostEstimate(flops=flops, bytes_accessed=bytes_accessed, transcendentals=0)


def pack_kernel(where, spatial_hbm, temporal_hbm, unit_a, unit_b, spatial, temporal, sem):
    core = where[3]
    half = pl.ds(pl.multiple_of(core * 32, 32), 32)
    copies = [
        pltpu.make_async_copy(spatial_hbm, spatial, sem.at[0]),
        pltpu.make_async_copy(temporal_hbm.at[:, half, :], temporal, sem.at[1]),
    ]
    for copy in copies:
        copy.start()
    source = lax.broadcasted_iota(jnp.int32, (256, 128), 0)
    target = lax.broadcasted_iota(jnp.int32, (256, 128), 1)
    wanted = (target >> 5) * 64 + (target & 31) + core * 32
    pick = jnp.where(source == wanted, 1.0, 0.0).astype(BF16)
    for copy in copies:
        copy.wait()
    for part in range(4):
        unit = (unit_a, unit_b)[part // 2]
        columns = spatial[:, :, part * 256 : (part + 1) * 256].reshape(576, 256)
        kept = jnp.dot(columns, pick, preferred_element_type=F32).astype(BF16)
        unit[0:576, (part % 2) * 128 : (part % 2 + 1) * 128] = kept
    for tap in range(3):
        rows = temporal[tap]
        for part in range(4):
            unit = (unit_a, unit_b)[part // 2]
            start = 576 + (part % 2) * 96 + tap * 32
            unit[start : start + 32, :] = rows[:, part * 256 : (part + 1) * 256]


def pack(where, spatial, temporal):
    unit = jax.ShapeDtypeStruct((768, 256), BF16)
    return pl.pallas_call(
        pack_kernel,
        out_shape=(unit, unit),
        in_specs=specs("s", "h", "h"),
        out_specs=specs("v", "v"),
        scratch_shapes=[
            pltpu.VMEM((9, 64, 1024), BF16),
            pltpu.VMEM((3, 32, 1024), BF16),
            pltpu.SemaphoreType.DMA((2,)),
        ],
        compiler_params=params(16),
        cost_estimate=cost(10**9, 3 * 10**6),
    )(where, spatial, temporal)


def norm_kernel(video, gain, active, flat, lines, plain):
    scale = gain[...]
    for i in range(ROWS):
        values = video[0, 0, i].astype(F32)
        mean = jnp.mean(values * values, axis=-1, keepdims=True)
        lines[i * COLS : (i + 1) * COLS, :] = silu(values * lax.rsqrt(mean + EPSILON) * scale)
        plain[i * COLS : (i + 1) * COLS, :] = values
    active[0] = lines[...].astype(BF16)
    flat[0] = plain[...].astype(BF16)


def norm(video, gain):
    return pl.pallas_call(
        norm_kernel,
        grid=(4,),
        out_shape=(jax.ShapeDtypeStruct((4, ROWS * COLS, 1024), BF16),) * 2,
        in_specs=[
            pl.BlockSpec((1, 1, ROWS, COLS, 1024), lambda i: (i // 2, i % 2, 0, 0, 0)),
            pl.BlockSpec((1, 1024), lambda i: (0, 0)),
        ],
        out_specs=(pl.BlockSpec((1, ROWS * COLS, 1024), lambda i: (i, 0, 0)),) * 2,
        scratch_shapes=[pltpu.VMEM((ROWS * COLS, 1024), F32)] * 2,
        compiler_params=params(24),
        cost_estimate=cost(2 * 10**9, 20 * 10**6),
    )(video, gain)


def spread_kernel(where, own, other, wide_a, wide_b, active):
    core = where[3]
    for relative, source in ((0, own), (1, other)):
        owner = core if relative == 0 else 1 - core
        for index in range(2):
            for frame in range(2):
                slot = (2 * owner + frame) * 2 + index
                for part in range(8):
                    values = source[index * 2 + frame, :, part * 128 : (part + 1) * 128]
                    active[part, pl.ds(slot, ROWS * COLS, stride=SLOTS), :] = values.astype(F32)

    low = lax.broadcasted_iota(jnp.int32, (LINE, 128), 1) < 64
    edge = jnp.zeros((SLOTS, 256), F32)

    def put(wide, block, i, value):
        wide[block, i + 1] = jnp.concatenate([edge, value, edge], axis=0).astype(BF16)

    def line(i, carry):
        lines = [active[part, pl.ds(i * LINE, LINE), :] for part in range(8)]
        for y in range(4):
            put(wide_b, y, i, jnp.concatenate([lines[2 * y], lines[2 * y + 1]], axis=1))
        turned = [pltpu.roll(value, 64, 1) for value in lines]
        for z in range(4):
            halves = []
            for y in (0, 2):
                first, second = y * 2 + z // 2, (y + 1) * 2 + z // 2
                if z % 2 == 0:
                    halves.append(jnp.where(low, lines[first], turned[second]))
                else:
                    halves.append(jnp.where(low, turned[first], lines[second]))
            put(wide_a, z, i, jnp.concatenate(halves, axis=1))
        return carry

    for block in range(4):
        for i in (0, ROWS + 1):
            for ref in (wide_a, wide_b):
                ref[block, i] = jnp.zeros(ref.shape[2:], BF16)
    lax.fori_loop(0, ROWS, line, 0)


def spread(where, own, other):
    wide = jax.ShapeDtypeStruct((4, ROWS + 2, LINE + 16, 256), BF16)
    return pl.pallas_call(
        spread_kernel,
        out_shape=(wide, wide),
        in_specs=specs("s", "v", "v"),
        out_specs=specs("v", "v"),
        scratch_shapes=[pltpu.VMEM((8, POINTS, 128), F32)],
        compiler_params=params(24),
        cost_estimate=cost(2 * 10**9, 25 * 10**6),
    )(where, own, other)


def stack_kernel(*refs):
    units, wholes = refs[:8], refs[8:]
    for index in range(8):
        wholes[index // 4][index % 4] = units[index][...]


def stack(units):
    whole = jax.ShapeDtypeStruct((4, 768, 256), BF16)
    return pl.pallas_call(
        stack_kernel,
        out_shape=(whole, whole),
        in_specs=specs(*"vvvvvvvv"),
        out_specs=specs(*"vv"),
        compiler_params=params(12),
        cost_estimate=cost(0, 6 * 10**6),
    )(*units)


def divide_kernel(whole_a, whole_b, spatial_a, spatial_b, temporal_a, temporal_b):
    for whole, spatial, temporal in ((whole_a, spatial_a, temporal_a), (whole_b, spatial_b, temporal_b)):
        for slot in range(4):
            spatial[slot] = whole[slot, 0:576, :]
            temporal[slot] = whole[slot, 576:768, :]


def divide(*wholes):
    spatial = jax.ShapeDtypeStruct((4, 576, 256), BF16)
    temporal = jax.ShapeDtypeStruct((4, 192, 256), BF16)
    return pl.pallas_call(
        divide_kernel,
        out_shape=(spatial, spatial, temporal, temporal),
        in_specs=specs(*"vv"),
        out_specs=specs(*"vvvv"),
        compiler_params=params(10),
        cost_estimate=cost(0, 6 * 10**6),
    )(*wholes)


def conv_kernel(step, colours, *refs):
    first, last = step == 0, step == 2
    count = len(colours)
    where, refs = refs[0], refs[1:]
    wide, refs = refs[:count], refs[count:]
    pieces, refs = refs[:count], refs[count:]
    if not first:
        sums, refs = refs[:count], refs[count:]
    if last:
        bias, refs = refs[0], refs[1:]
        if colours[0] > 0:
            earlier, refs = refs[:2], refs[2:]
        hidden, lower, upper, kernel, sides = refs
        if colours[0] > 0:
            for ref, source in zip((lower, upper), earlier):
                ref[0] = source[0]
    else:
        out, kernel = refs[:count], refs[count]
    y, z = where[0], where[1]
    turn = 2 * where[3] - 1
    mine = (z, y)
    across = (y, z)
    lines = 6
    for number, colour in enumerate(colours):
        block = (mine[colour] + turn * step + 4) & 3
        for slot in range(4):
            place = (across[colour] + turn * slot + 4) & 3
            for tap in range(9):
                kernel[number, pl.ds(pl.multiple_of(tap * 256 + place * 64, 64), 64), :] = pieces[number][
                    slot, tap * 64 : (tap + 1) * 64, :
                ]

        def part(group, carry, number=number, colour=colour, block=block):
            i = group * lines
            total = None
            for tap in range(9):
                dy, dx = tap // 3, tap % 3
                window = wide[number][block, pl.ds(i + dy, lines), dx * 8 : dx * 8 + LINE, :]
                product = jnp.dot(
                    window.reshape(lines * LINE, 256),
                    kernel[number, tap * 256 : (tap + 1) * 256, :],
                    preferred_element_type=F32,
                )
                total = product if total is None else total + product
            rows = pl.ds(pl.multiple_of(i * LINE, lines * LINE), lines * LINE)
            if not first:
                total = total + sums[number][rows, :]
            if last:
                total = silu(total + bias[:, colour * 256 : (colour + 1) * 256])
                hidden[rows, :] = total.astype(BF16)
                for half in range(2):
                    sides[half, rows, :] = total[:, half * 128 : (half + 1) * 128]
            else:
                out[number][rows, :] = total
            return carry

        lax.fori_loop(0, ROWS // lines, part, 0)
        if last:
            for half in range(2):
                columns = slice(half * 128, (half + 1) * 128)
                for index in range(2):
                    for ref, slot in ((lower, index), (upper, 6 + index)):
                        values = sides[half, pl.ds(slot, ROWS * COLS, stride=SLOTS), :]
                        ref[colour, index, :, columns] = values.astype(BF16)


def conv(step, colours, where, active, spatial, sums=None, bias=None, sides=()):
    count = len(colours)
    operands = [where, *active, *spatial]
    kinds = "s" + "vv" * count
    scratch = [pltpu.VMEM((count, 2304, 256), BF16)]
    aliases = {}
    if step > 0:
        if step != 2:
            aliases = {len(operands) + number: number for number in range(count)}
        operands += sums
        kinds += "v" * count
    if step == 2:
        operands.append(bias)
        kinds += "v"
        operands += sides
        kinds += "v" * len(sides)
        side = jax.ShapeDtypeStruct((2, 2, ROWS * COLS, 256), BF16)
        out_shape = (jax.ShapeDtypeStruct((POINTS, 256), BF16), side, side)
        out_specs = specs(*"vvv")
        scratch += [pltpu.VMEM((2, POINTS, 128), F32)]
    else:
        total = jax.ShapeDtypeStruct((POINTS, 256), F32)
        out_shape, out_specs = (total,) * count, specs(*"v" * count)
    return pl.pallas_call(
        functools.partial(conv_kernel, step, colours),
        out_shape=out_shape,
        in_specs=specs(*kinds),
        out_specs=out_specs,
        scratch_shapes=scratch,
        input_output_aliases=aliases,
        compiler_params=params(16),
        cost_estimate=cost(4 * 10**9 * count, 12 * 10**6 * count),
    )(*operands)


def shift_kernel(hidden_a, hidden_b, earlier, later):
    slot = lax.broadcasted_iota(jnp.int32, (LINE, 128), 0) & 7
    for part in range(4):
        source, columns = (hidden_a, hidden_b)[part // 2], slice(part % 2 * 128, (part % 2 + 1) * 128)

        def move(i, carry, source=source, columns=columns, part=part):
            rows = pl.ds(pl.multiple_of(i * LINE, LINE), LINE)
            values = source[rows, columns].astype(F32)
            target = slice(part * 128, (part + 1) * 128)
            earlier[rows, target] = jnp.where(slot >= 2, pltpu.roll(values, 2, 0), 0.0).astype(BF16)
            later[rows, target] = jnp.where(slot < 6, pltpu.roll(values, LINE - 2, 0), 0.0).astype(BF16)
            return carry

        lax.fori_loop(0, ROWS, move, 0)


def shift(hidden):
    moved = jax.ShapeDtypeStruct((POINTS, 512), BF16)
    return pl.pallas_call(
        shift_kernel,
        out_shape=(moved, moved),
        in_specs=specs("v", "v"),
        out_specs=specs("v", "v"),
        compiler_params=params(16),
        cost_estimate=cost(10**9, 6 * 10**6),
    )(*hidden)


def place_weights(where, blocks, steps, first_row, targets):
    y, z = where[0], where[1]
    turn = 2 * where[3] - 1
    for number, ref in enumerate(blocks):
        colour, step = number % 2, steps[number // 2]
        for unit in range(4):
            fixed, moving = (unit, step) if colour == 0 else (step, unit)
            row, column = (y + turn * fixed + 4) & 3, (z + turn * moving + 4) & 3
            place = pl.ds(pl.multiple_of((row * 4 + column) * 32, 32), 32)
            for half in range(2):
                columns = slice((colour * 2 + half) * 256, (colour * 2 + half + 1) * 256)
                start = first_row + half * 96
                for tap, target in enumerate(targets):
                    target[place, columns] = ref[unit, start + tap * 32 : start + tap * 32 + 32, :]


def ready_kernel(where, *refs):
    blocks, weights = refs[:6], refs[6]
    place_weights(where, blocks, (0, 1, 3), 576, [weights.at[tap] for tap in range(3)])


def ready(where, blocks):
    return pl.pallas_call(
        ready_kernel,
        out_shape=jax.ShapeDtypeStruct((3, 512, 1024), BF16),
        in_specs=specs(*"svvvvvv"),
        out_specs=pl.BlockSpec(memory_space=pltpu.VMEM),
        compiler_params=params(18),
        cost_estimate=cost(0, 5 * 10**6),
    )(where, *blocks)


def centre_kernel(where, hidden_a, hidden_b, earlier, later, weights, block_a, block_b, *refs):
    calm_theirs, calm_mine, rough_theirs, rough_mine, edge, middle, total = refs
    core = where[3]
    edge[0], middle[...], edge[1] = weights[0], weights[1], weights[2]
    place_weights(where, (block_a, block_b), (2,), 0, (edge.at[0], middle, edge.at[1]))
    for part in range(4):
        columns = slice(part * 256, (part + 1) * 256)
        for group in range(2):
            rows = slice(group * 960, (group + 1) * 960)
            value = jnp.dot(hidden_a[rows, :], middle[0:256, columns], preferred_element_type=F32)
            value = value + jnp.dot(hidden_b[rows, :], middle[256:512, columns], preferred_element_type=F32)
            value = value + jnp.dot(earlier[rows, :], edge[0, :, columns], preferred_element_type=F32)
            value = value + jnp.dot(later[rows, :], edge[1, :, columns], preferred_element_type=F32)
            for half in range(2):
                total[part * 2 + half, rows, :] = value[:, half * 128 : (half + 1) * 128]
        for index in range(2):
            for target, owner, frame in (
                (calm_theirs, 1 - core, core),
                (rough_theirs, 1 - core, 1 - core),
                (calm_mine, core, 1 - core),
                (rough_mine, core, core),
            ):
                start = (2 * owner + frame) * 2 + index
                for half in (part * 2, part * 2 + 1):
                    values = total[half, pl.ds(start, ROWS * COLS, stride=SLOTS), :]
                    target[index, :, half * 128 : (half + 1) * 128] = values.astype(target.dtype)


PAIR = (2, ROWS * COLS, 1024)


def centre(where, hidden, moved, weights, blocks):
    wide, narrow = jax.ShapeDtypeStruct(PAIR, F32), jax.ShapeDtypeStruct(PAIR, BF16)
    return pl.pallas_call(
        centre_kernel,
        out_shape=(narrow, wide, wide, wide, jax.ShapeDtypeStruct((2, 512, 1024), BF16)),
        in_specs=specs(*"svvvvvvv"),
        out_specs=specs(*"vvvvv"),
        scratch_shapes=[pltpu.VMEM((512, 1024), BF16), pltpu.VMEM((8, POINTS, 128), F32)],
        compiler_params=params(32),
        cost_estimate=cost(10**10, 12 * 10**6),
    )(where, *hidden, *moved, weights, *blocks)


def edge_kernel(own, where, before, behind, weights, calm, result):
    core = where[3]
    for side, halo in enumerate((before, behind)):

        @pl.when(core == side if own else core != side)
        def _(side=side, halo=halo):
            for index in range(2):
                value = jnp.dot(halo[0, index], weights[side, 0:256, :], preferred_element_type=F32)
                value = value + jnp.dot(halo[1, index], weights[side, 256:512, :], preferred_element_type=F32)
                result[index] = (calm[index] + value).astype(result.dtype)


def edges(own, where, before, behind, weights, calm):
    return pl.pallas_call(
        functools.partial(edge_kernel, own),
        out_shape=jax.ShapeDtypeStruct(PAIR, F32 if own else BF16),
        in_specs=specs(*"svvvv"),
        out_specs=pl.BlockSpec(memory_space=pltpu.VMEM),
        compiler_params=params(24),
        cost_estimate=cost(3 * 10**9, 6 * 10**6),
    )(where, before, behind, weights, calm)


def finish_kernel(where, video, calm_mine, calm_received, rough_mine, rough_received, result, lines):
    core, index = where[3], pl.program_id(0)
    for part in range(8):
        columns = slice(part * 128, (part + 1) * 128)
        for frame, mine, received in (
            (core, rough_mine, rough_received),
            (1 - core, calm_mine, calm_received),
        ):
            value = video[2 * index + frame, :, columns].astype(F32) + (
                mine[index, :, columns] + received[index, :, columns].astype(F32)
            )
            lines[part, pl.ds(frame, ROWS * COLS, stride=2), :] = value
        for i in range(ROWS):
            value = lines[part, i * 2 * COLS : (i + 1) * 2 * COLS, :]
            result[0, i, :, :, columns] = value.astype(BF16).reshape(COLS, 2, 128)


def finish(where, video, *parts):
    shown = pl.pallas_call(
        finish_kernel,
        grid=(2,),
        out_shape=jax.ShapeDtypeStruct((2, ROWS, COLS, 2, 1024), BF16),
        in_specs=specs(*"svvvvv"),
        out_specs=pl.BlockSpec((1, ROWS, COLS, 2, 1024), lambda i: (i, 0, 0, 0, 0)),
        scratch_shapes=[pltpu.VMEM((8, 2 * ROWS * COLS, 128), F32)],
        compiler_params=params(24),
        cost_estimate=cost(3 * 10**6, 10 * 10**6),
    )(where, video, *parts)
    return shown.transpose(0, 3, 1, 2, 4)


def ring(value, axis, way=1):
    count = lax.axis_size(axis)
    pairs = [(i * 2, (i + way) % count * 2) for i in range(count)]
    pairs += [(i * 2 + 1, (i - way) % count * 2 + 1) for i in range(count)]
    return lax.ppermute(value, (axis, "core"), pairs)


def after(value, *others):
    return lax.optimization_barrier((value, *others))[0]


def shards(video, norm_gain, spatial_weight, spatial_bias, temporal_weight):
    where = jnp.stack([lax.axis_index(axis) for axis in ("y", "z", "x", "core")]).astype(jnp.int32)
    swap = [(0, 1), (1, 0)]
    bias = spatial_bias.reshape(16, 2, 32)[:, where[3], :].reshape(1, 512)
    unit_a, unit_b = pack(where, spatial_weight, temporal_weight)

    a1, b1 = ring(unit_a, "y"), ring(unit_b, "z")
    a3, b3 = ring(unit_a, "y", -1), ring(unit_b, "z", -1)
    a2, b2 = ring(a1, "y"), ring(b1, "z")
    own, flat = norm(after(video, a1, b1, bias), norm_gain.reshape(1, 1024))
    other = lax.ppermute(after(own, a2, b2, a3, b3), "core", swap)
    whole_a, whole_b = stack((unit_a, a1, after(a2, own), a3, unit_b, b1, b2, b3))

    both = (0, 1)
    whole_1 = ring(whole_a, "z"), ring(whole_b, "y")
    active = spread(where, after(own, whole_a), other)
    whole_3 = ring(after(whole_a, active[0]), "z", -1), ring(after(whole_b, active[0]), "y", -1)
    sums = conv(0, both, where, active, (whole_a, whole_b))
    sa, sb, ta, tb = divide(after(whole_1[0], sums[0]), whole_1[1])
    sa, sb = ring(sa, "z"), ring(sb, "y")
    sums = conv(1, both, where, active, whole_1, sums)
    ta, tb = ring(after(ta, *whole_3), "z"), ring(after(tb, *whole_3), "y")
    sums = conv(3, both, where, active, whole_3, sums)
    weights = ready(where, (whole_a, whole_b, *whole_1, *whole_3))
    sa, sb = after(sa, sums[0], weights), after(sb, sums[0], weights)
    hidden_a, *sides = conv(2, (0,), where, active[:1], (sa,), sums[:1], bias)
    hidden_b, lower, upper = conv(2, (1,), where, active[1:], (sb,), sums[1:], bias, sides)
    count = lax.axis_size("x")
    before = lax.ppermute(upper, "x", [(i, i + 1) for i in range(count - 1)])
    behind = lax.ppermute(lower, "x", [(i + 1, i) for i in range(count - 1)])
    hidden = hidden_a, hidden_b
    moved = shift(hidden)
    calm_theirs, calm_mine, rough_theirs, rough_mine, weights = centre(where, hidden, moved, weights, (ta, tb))
    calm_received = lax.ppermute(calm_theirs, "core", swap)
    before = after(before, weights)
    sent = edges(False, where, before, behind, weights, rough_theirs)
    rough_received = lax.ppermute(sent, "core", swap)
    rough_mine = edges(True, where, before, behind, weights, after(rough_mine, sent))
    return finish(where, flat, calm_mine, calm_received, rough_mine, rough_received)


def solution(mesh):
    parts = Mesh(mesh.devices.reshape(4, 4, 4, 2), ("y", "z", "x", "core"))
    dp, frame = ("y", "z"), ("x", "core")
    in_specs = (
        P(dp, frame, None, None, None),
        P(),
        P(None, dp, None),
        P(),
        P(None, dp, None),
    )
    out_specs = P(dp, frame, None, None, None)
    return jax.shard_map(shards, mesh=parts, in_specs=in_specs, out_specs=out_specs, check_vma=False)
```

```python
import functools

import jax
import jax.numpy as jnp
from jax import lax
from jax.experimental import pallas as pl
from jax.experimental.pallas import tpu as pltpu
from jax.sharding import Mesh
from jax.sharding import PartitionSpec as P

EPSILON = 1e-06
F32, BF16 = jnp.float32, jnp.bfloat16
MIB = 2**20

ROWS, COLS, SLOTS = 12, 20, 8
LINE = COLS * SLOTS
POINTS = ROWS * LINE


def silu(v):
    return v / (1.0 + jnp.exp(-v))


def specs(*kinds):
    places = {"s": pltpu.SMEM, "v": pltpu.VMEM, "h": pltpu.HBM}
    return [pl.BlockSpec(memory_space=places[kind]) for kind in kinds]


def params(mib):
    return pltpu.CompilerParams(vmem_limit_bytes=mib * MIB)


def cost(flops, bytes_accessed):
    return pl.CostEstimate(flops=flops, bytes_accessed=bytes_accessed, transcendentals=0)


def pack_kernel(where, spatial, temporal, unit_a, unit_b):
    core = where[3]
    source = lax.broadcasted_iota(jnp.int32, (256, 128), 0)
    target = lax.broadcasted_iota(jnp.int32, (256, 128), 1)
    wanted = (target >> 5) * 64 + (target & 31) + core * 32
    pick = jnp.where(source == wanted, 1.0, 0.0).astype(BF16)
    for part in range(4):
        unit = (unit_a, unit_b)[part // 2]
        columns = spatial[:, :, part * 256 : (part + 1) * 256].reshape(576, 256)
        kept = jnp.dot(columns, pick, preferred_element_type=F32).astype(BF16)
        unit[0:576, (part % 2) * 128 : (part % 2 + 1) * 128] = kept
    for tap in range(3):
        rows = temporal[tap, pl.ds(pl.multiple_of(core * 32, 32), 32), :]
        for part in range(4):
            unit = (unit_a, unit_b)[part // 2]
            start = 576 + (part % 2) * 96 + tap * 32
            unit[start : start + 32, :] = rows[:, part * 256 : (part + 1) * 256]


def pack(where, spatial, temporal):
    unit = jax.ShapeDtypeStruct((768, 256), BF16)
    return pl.pallas_call(
        pack_kernel,
        out_shape=(unit, unit),
        in_specs=specs("s", "v", "v"),
        out_specs=specs("v", "v"),
        compiler_params=params(16),
        cost_estimate=cost(10**9, 3 * 10**6),
    )(where, spatial, temporal)


def norm_kernel(video, gain, active, flat, lines, plain):
    scale = gain[...]
    for i in range(ROWS):
        values = video[0, 0, i].astype(F32)
        mean = jnp.mean(values * values, axis=-1, keepdims=True)
        lines[i * COLS : (i + 1) * COLS, :] = silu(values * lax.rsqrt(mean + EPSILON) * scale)
        plain[i * COLS : (i + 1) * COLS, :] = values
    active[0] = lines[...].astype(BF16)
    flat[0] = plain[...].astype(BF16)


def norm(video, gain):
    return pl.pallas_call(
        norm_kernel,
        grid=(4,),
        out_shape=(jax.ShapeDtypeStruct((4, ROWS * COLS, 1024), BF16),) * 2,
        in_specs=[
            pl.BlockSpec((1, 1, ROWS, COLS, 1024), lambda i: (i // 2, i % 2, 0, 0, 0)),
            pl.BlockSpec((1, 1024), lambda i: (0, 0)),
        ],
        out_specs=(pl.BlockSpec((1, ROWS * COLS, 1024), lambda i: (i, 0, 0)),) * 2,
        scratch_shapes=[pltpu.VMEM((ROWS * COLS, 1024), F32)] * 2,
        compiler_params=params(24),
        cost_estimate=cost(2 * 10**9, 20 * 10**6),
    )(video, gain)


def spread_kernel(where, own, other, wide_a, wide_b, active):
    core = where[3]
    for relative, source in ((0, own), (1, other)):
        owner = core if relative == 0 else 1 - core
        for index in range(2):
            for frame in range(2):
                slot = (2 * owner + frame) * 2 + index
                for part in range(8):
                    values = source[index * 2 + frame, :, part * 128 : (part + 1) * 128]
                    active[part, pl.ds(slot, ROWS * COLS, stride=SLOTS), :] = values.astype(F32)

    low = lax.broadcasted_iota(jnp.int32, (LINE, 128), 1) < 64
    edge = jnp.zeros((SLOTS, 256), F32)

    def put(wide, block, i, value):
        wide[block, i + 1] = jnp.concatenate([edge, value, edge], axis=0).astype(BF16)

    def line(i, carry):
        lines = [active[part, pl.ds(i * LINE, LINE), :] for part in range(8)]
        for y in range(4):
            put(wide_b, y, i, jnp.concatenate([lines[2 * y], lines[2 * y + 1]], axis=1))
        turned = [pltpu.roll(value, 64, 1) for value in lines]
        for z in range(4):
            halves = []
            for y in (0, 2):
                first, second = y * 2 + z // 2, (y + 1) * 2 + z // 2
                if z % 2 == 0:
                    halves.append(jnp.where(low, lines[first], turned[second]))
                else:
                    halves.append(jnp.where(low, turned[first], lines[second]))
            put(wide_a, z, i, jnp.concatenate(halves, axis=1))
        return carry

    for block in range(4):
        for i in (0, ROWS + 1):
            for ref in (wide_a, wide_b):
                ref[block, i] = jnp.zeros(ref.shape[2:], BF16)
    lax.fori_loop(0, ROWS, line, 0)


def spread(where, own, other):
    wide = jax.ShapeDtypeStruct((4, ROWS + 2, LINE + 16, 256), BF16)
    return pl.pallas_call(
        spread_kernel,
        out_shape=(wide, wide),
        in_specs=specs("s", "v", "v"),
        out_specs=specs("v", "v"),
        scratch_shapes=[pltpu.VMEM((8, POINTS, 128), F32)],
        compiler_params=params(24),
        cost_estimate=cost(2 * 10**9, 25 * 10**6),
    )(where, own, other)


def stack_kernel(*refs):
    units, wholes = refs[:8], refs[8:]
    for index in range(8):
        wholes[index // 4][index % 4] = units[index][...]


def stack(units):
    whole = jax.ShapeDtypeStruct((4, 768, 256), BF16)
    return pl.pallas_call(
        stack_kernel,
        out_shape=(whole, whole),
        in_specs=specs(*"vvvvvvvv"),
        out_specs=specs(*"vv"),
        compiler_params=params(12),
        cost_estimate=cost(0, 6 * 10**6),
    )(*units)


def divide_kernel(whole_a, whole_b, spatial_a, spatial_b, temporal_a, temporal_b):
    for whole, spatial, temporal in ((whole_a, spatial_a, temporal_a), (whole_b, spatial_b, temporal_b)):
        for slot in range(4):
            spatial[slot] = whole[slot, 0:576, :]
            temporal[slot] = whole[slot, 576:768, :]


def divide(*wholes):
    spatial = jax.ShapeDtypeStruct((4, 576, 256), BF16)
    temporal = jax.ShapeDtypeStruct((4, 192, 256), BF16)
    return pl.pallas_call(
        divide_kernel,
        out_shape=(spatial, spatial, temporal, temporal),
        in_specs=specs(*"vv"),
        out_specs=specs(*"vvvv"),
        compiler_params=params(10),
        cost_estimate=cost(0, 6 * 10**6),
    )(*wholes)


def conv_kernel(step, colours, *refs):
    first, last = step == 0, step == 2
    count = len(colours)
    where, refs = refs[0], refs[1:]
    wide, refs = refs[:count], refs[count:]
    pieces, refs = refs[:count], refs[count:]
    if not first:
        sums, refs = refs[:count], refs[count:]
    if last:
        bias, refs = refs[0], refs[1:]
        if colours[0] > 0:
            earlier, refs = refs[:2], refs[2:]
        hidden, lower, upper, kernel, sides = refs
        if colours[0] > 0:
            for ref, source in zip((lower, upper), earlier):
                ref[0] = source[0]
    else:
        out, kernel = refs[:count], refs[count]
    y, z = where[0], where[1]
    turn = 2 * where[3] - 1
    mine = (z, y)
    across = (y, z)
    lines = 6
    for number, colour in enumerate(colours):
        block = (mine[colour] + turn * step + 4) & 3
        for slot in range(4):
            place = (across[colour] + turn * slot + 4) & 3
            for tap in range(9):
                kernel[number, pl.ds(pl.multiple_of(tap * 256 + place * 64, 64), 64), :] = pieces[number][
                    slot, tap * 64 : (tap + 1) * 64, :
                ]

        def part(group, carry, number=number, colour=colour, block=block):
            i = group * lines
            total = None
            for tap in range(9):
                dy, dx = tap // 3, tap % 3
                window = wide[number][block, pl.ds(i + dy, lines), dx * 8 : dx * 8 + LINE, :]
                product = jnp.dot(
                    window.reshape(lines * LINE, 256),
                    kernel[number, tap * 256 : (tap + 1) * 256, :],
                    preferred_element_type=F32,
                )
                total = product if total is None else total + product
            rows = pl.ds(pl.multiple_of(i * LINE, lines * LINE), lines * LINE)
            if not first:
                total = total + sums[number][rows, :]
            if last:
                total = silu(total + bias[:, colour * 256 : (colour + 1) * 256])
                hidden[rows, :] = total.astype(BF16)
                for half in range(2):
                    sides[half, rows, :] = total[:, half * 128 : (half + 1) * 128]
            else:
                out[number][rows, :] = total
            return carry

        lax.fori_loop(0, ROWS // lines, part, 0)
        if last:
            for half in range(2):
                columns = slice(half * 128, (half + 1) * 128)
                for index in range(2):
                    for ref, slot in ((lower, index), (upper, 6 + index)):
                        values = sides[half, pl.ds(slot, ROWS * COLS, stride=SLOTS), :]
                        ref[colour, index, :, columns] = values.astype(BF16)


def conv(step, colours, where, active, spatial, sums=None, bias=None, sides=()):
    count = len(colours)
    operands = [where, *active, *spatial]
    kinds = "s" + "vv" * count
    scratch = [pltpu.VMEM((count, 2304, 256), BF16)]
    aliases = {}
    if step > 0:
        if step != 2:
            aliases = {len(operands) + number: number for number in range(count)}
        operands += sums
        kinds += "v" * count
    if step == 2:
        operands.append(bias)
        kinds += "v"
        operands += sides
        kinds += "v" * len(sides)
        side = jax.ShapeDtypeStruct((2, 2, ROWS * COLS, 256), BF16)
        out_shape = (jax.ShapeDtypeStruct((POINTS, 256), BF16), side, side)
        out_specs = specs(*"vvv")
        scratch += [pltpu.VMEM((2, POINTS, 128), F32)]
    else:
        total = jax.ShapeDtypeStruct((POINTS, 256), F32)
        out_shape, out_specs = (total,) * count, specs(*"v" * count)
    return pl.pallas_call(
        functools.partial(conv_kernel, step, colours),
        out_shape=out_shape,
        in_specs=specs(*kinds),
        out_specs=out_specs,
        scratch_shapes=scratch,
        input_output_aliases=aliases,
        compiler_params=params(16),
        cost_estimate=cost(4 * 10**9 * count, 12 * 10**6 * count),
    )(*operands)


def shift_kernel(hidden_a, hidden_b, earlier, later):
    slot = lax.broadcasted_iota(jnp.int32, (LINE, 128), 0) & 7
    for part in range(4):
        source, columns = (hidden_a, hidden_b)[part // 2], slice(part % 2 * 128, (part % 2 + 1) * 128)

        def move(i, carry, source=source, columns=columns, part=part):
            rows = pl.ds(pl.multiple_of(i * LINE, LINE), LINE)
            values = source[rows, columns].astype(F32)
            target = slice(part * 128, (part + 1) * 128)
            earlier[rows, target] = jnp.where(slot >= 2, pltpu.roll(values, 2, 0), 0.0).astype(BF16)
            later[rows, target] = jnp.where(slot < 6, pltpu.roll(values, LINE - 2, 0), 0.0).astype(BF16)
            return carry

        lax.fori_loop(0, ROWS, move, 0)


def shift(hidden):
    moved = jax.ShapeDtypeStruct((POINTS, 512), BF16)
    return pl.pallas_call(
        shift_kernel,
        out_shape=(moved, moved),
        in_specs=specs("v", "v"),
        out_specs=specs("v", "v"),
        compiler_params=params(16),
        cost_estimate=cost(10**9, 6 * 10**6),
    )(*hidden)


def place_weights(where, blocks, targets):
    y, z = where[0], where[1]
    turn = 2 * where[3] - 1
    for number, ref in enumerate(blocks):
        colour, step = number % 2, number // 2
        first_row = 0 if step == 2 else 576
        for unit in range(4):
            fixed, moving = (unit, step) if colour == 0 else (step, unit)
            row, column = (y + turn * fixed + 4) & 3, (z + turn * moving + 4) & 3
            place = pl.ds(pl.multiple_of((row * 4 + column) * 32, 32), 32)
            for half in range(2):
                columns = slice((colour * 2 + half) * 256, (colour * 2 + half + 1) * 256)
                start = first_row + half * 96
                for tap, target in enumerate(targets):
                    target[place, columns] = ref[unit, start + tap * 32 : start + tap * 32 + 32, :]


def centre_kernel(where, hidden_a, hidden_b, earlier, later, *refs):
    blocks, (calm_theirs, calm_mine, rough_theirs, rough_mine, edge, middle, total) = refs[:8], refs[8:]
    core = where[3]
    place_weights(where, blocks, (edge.at[0], middle, edge.at[1]))
    for part in range(4):
        columns = slice(part * 256, (part + 1) * 256)
        for group in range(2):
            rows = slice(group * 960, (group + 1) * 960)
            value = jnp.dot(hidden_a[rows, :], middle[0:256, columns], preferred_element_type=F32)
            value = value + jnp.dot(hidden_b[rows, :], middle[256:512, columns], preferred_element_type=F32)
            value = value + jnp.dot(earlier[rows, :], edge[0, :, columns], preferred_element_type=F32)
            value = value + jnp.dot(later[rows, :], edge[1, :, columns], preferred_element_type=F32)
            for half in range(2):
                total[part * 2 + half, rows, :] = value[:, half * 128 : (half + 1) * 128]
        for index in range(2):
            for target, owner, frame in (
                (calm_theirs, 1 - core, core),
                (rough_theirs, 1 - core, 1 - core),
                (calm_mine, core, 1 - core),
                (rough_mine, core, core),
            ):
                start = (2 * owner + frame) * 2 + index
                for half in (part * 2, part * 2 + 1):
                    values = total[half, pl.ds(start, ROWS * COLS, stride=SLOTS), :]
                    target[index, :, half * 128 : (half + 1) * 128] = values.astype(target.dtype)


PAIR = (2, ROWS * COLS, 1024)


def centre(where, hidden, moved, blocks):
    wide, narrow = jax.ShapeDtypeStruct(PAIR, F32), jax.ShapeDtypeStruct(PAIR, BF16)
    return pl.pallas_call(
        centre_kernel,
        out_shape=(narrow, wide, wide, wide, jax.ShapeDtypeStruct((2, 512, 1024), BF16)),
        in_specs=specs(*"svvvv", *"vvvvvvvv"),
        out_specs=specs(*"vvvvv"),
        scratch_shapes=[pltpu.VMEM((512, 1024), BF16), pltpu.VMEM((8, POINTS, 128), F32)],
        compiler_params=params(20),
        cost_estimate=cost(10**10, 12 * 10**6),
    )(where, *hidden, *moved, *blocks)


def edge_kernel(own, where, before, behind, weights, calm, result):
    core = where[3]
    for side, halo in enumerate((before, behind)):

        @pl.when(core == side if own else core != side)
        def _(side=side, halo=halo):
            for index in range(2):
                value = jnp.dot(halo[0, index], weights[side, 0:256, :], preferred_element_type=F32)
                value = value + jnp.dot(halo[1, index], weights[side, 256:512, :], preferred_element_type=F32)
                result[index] = (calm[index] + value).astype(result.dtype)


def edges(own, where, before, behind, weights, calm):
    return pl.pallas_call(
        functools.partial(edge_kernel, own),
        out_shape=jax.ShapeDtypeStruct(PAIR, F32 if own else BF16),
        in_specs=specs(*"svvvv"),
        out_specs=pl.BlockSpec(memory_space=pltpu.VMEM),
        compiler_params=params(24),
        cost_estimate=cost(3 * 10**9, 6 * 10**6),
    )(where, before, behind, weights, calm)


def finish_kernel(where, video, calm_mine, calm_received, rough_mine, rough_received, result, lines):
    core, index = where[3], pl.program_id(0)
    for part in range(8):
        columns = slice(part * 128, (part + 1) * 128)
        for frame, mine, received in (
            (core, rough_mine, rough_received),
            (1 - core, calm_mine, calm_received),
        ):
            value = video[2 * index + frame, :, columns].astype(F32) + (
                mine[index, :, columns] + received[index, :, columns].astype(F32)
            )
            lines[part, pl.ds(frame, ROWS * COLS, stride=2), :] = value
        for i in range(ROWS):
            value = lines[part, i * 2 * COLS : (i + 1) * 2 * COLS, :]
            result[0, i, :, :, columns] = value.astype(BF16).reshape(COLS, 2, 128)


def finish(where, video, *parts):
    shown = pl.pallas_call(
        finish_kernel,
        grid=(2,),
        out_shape=jax.ShapeDtypeStruct((2, ROWS, COLS, 2, 1024), BF16),
        in_specs=specs(*"svvvvv"),
        out_specs=pl.BlockSpec((1, ROWS, COLS, 2, 1024), lambda i: (i, 0, 0, 0, 0)),
        scratch_shapes=[pltpu.VMEM((8, 2 * ROWS * COLS, 128), F32)],
        compiler_params=params(24),
        cost_estimate=cost(3 * 10**6, 10 * 10**6),
    )(where, video, *parts)
    return shown.transpose(0, 3, 1, 2, 4)


def ring(value, axis, way=1):
    count = lax.axis_size(axis)
    pairs = [(i * 2, (i + way) % count * 2) for i in range(count)]
    pairs += [(i * 2 + 1, (i - way) % count * 2 + 1) for i in range(count)]
    return lax.ppermute(value, (axis, "core"), pairs)


def after(value, *others):
    return lax.optimization_barrier((value, *others))[0]


def shards(video, norm_gain, spatial_weight, spatial_bias, temporal_weight):
    where = jnp.stack([lax.axis_index(axis) for axis in ("y", "z", "x", "core")]).astype(jnp.int32)
    swap = [(0, 1), (1, 0)]
    bias = spatial_bias.reshape(16, 2, 32)[:, where[3], :].reshape(1, 512)
    unit_a, unit_b = pack(where, spatial_weight, temporal_weight)

    a1, b1 = ring(unit_a, "y"), ring(unit_b, "z")
    a3, b3 = ring(unit_a, "y", -1), ring(unit_b, "z", -1)
    a2, b2 = ring(a1, "y"), ring(b1, "z")
    own, flat = norm(after(video, a1, b1, bias), norm_gain.reshape(1, 1024))
    other = lax.ppermute(after(own, a2, b2, a3, b3), "core", swap)
    whole_a, whole_b = stack((unit_a, a1, after(a2, own), a3, unit_b, b1, b2, b3))

    both = (0, 1)
    whole_1 = ring(whole_a, "z"), ring(whole_b, "y")
    active = spread(where, after(own, whole_a), other)
    whole_3 = ring(after(whole_a, active[0]), "z", -1), ring(after(whole_b, active[0]), "y", -1)
    sums = conv(0, both, where, active, (whole_a, whole_b))
    sa, sb, ta, tb = divide(after(whole_1[0], sums[0]), whole_1[1])
    sa, sb = ring(sa, "z"), ring(sb, "y")
    sums = conv(1, both, where, active, whole_1, sums)
    (sum_a,) = conv(3, (0,), where, active[:1], whole_3[:1], sums[:1])
    ta, tb = ring(after(ta, *whole_3, sum_a), "z"), ring(after(tb, *whole_3, sum_a), "y")
    (sum_b,) = conv(3, (1,), where, active[1:], whole_3[1:], sums[1:])
    sums = [sum_a, sum_b]
    sa, sb = after(sa, *sums), after(sb, *sums)
    hidden_a, *sides = conv(2, (0,), where, active[:1], (sa,), sums[:1], bias)
    hidden_b, lower, upper = conv(2, (1,), where, active[1:], (sb,), sums[1:], bias, sides)
    count = lax.axis_size("x")
    before = lax.ppermute(upper, "x", [(i, i + 1) for i in range(count - 1)])
    behind = lax.ppermute(lower, "x", [(i + 1, i) for i in range(count - 1)])
    hidden = hidden_a, hidden_b
    moved = shift(hidden)
    calm_theirs, calm_mine, rough_theirs, rough_mine, weights = centre(
        where, hidden, moved, (whole_a, whole_b, *whole_1, ta, tb, *whole_3)
    )
    calm_received = lax.ppermute(calm_theirs, "core", swap)
    before = after(before, weights)
    sent = edges(False, where, before, behind, weights, rough_theirs)
    rough_received = lax.ppermute(sent, "core", swap)
    rough_mine = edges(True, where, before, behind, weights, after(rough_mine, sent))
    return finish(where, flat, calm_mine, calm_received, rough_mine, rough_received)


def solution(mesh):
    parts = Mesh(mesh.devices.reshape(4, 4, 4, 2), ("y", "z", "x", "core"))
    dp, frame = ("y", "z"), ("x", "core")
    in_specs = (
        P(dp, frame, None, None, None),
        P(),
        P(None, dp, None),
        P(),
        P(None, dp, None),
    )
    out_specs = P(dp, frame, None, None, None)
    return jax.shard_map(shards, mesh=parts, in_specs=in_specs, out_specs=out_specs, check_vma=False)
```
